32 devices in a mesh: groups: 2 (over y), seq: 4 (over z), head: 2 (over x), sub: 2 (over core).
Axes of the slice: x: 2, y: 2, z: 4, core: 2. Of those that a mesh axis runs over, the one named last changes fastest.
Arguments:
- query_rows: bfloat16 [32, 128, 8192], P('head', 'sub', ('groups', 'seq')), parts along dimension 2, may hold values from -6 to 6
- key_rows: bfloat16 [32, 128, 8192], P('head', 'sub', ('groups', 'seq')), parts along dimension 2, may hold values from -0.5 to 0.5
- value_rows: bfloat16 [32, 64, 8192], P('head', None, ('groups', 'seq')), parts along dimension 2, may hold values from -6 to 6
- level_weights: bfloat16 [32, 7, 8192], P('head', None, ('groups', 'seq')), parts along dimension 2, may hold values from 0.29882812 to 3
Outputs:
- mixed_output: bfloat16 [32, 64, 8192], P('head', 'sub', ('groups', 'seq')), parts along dimension 2
The draws below stay inside these ranges and needn't reach their ends.
There are 2 independent parts, one for each index of `groups`. The reference program is written for one: setup_inputs(seed, part) draws one part's arguments, and reference() takes and returns one part's arrays. A program takes and returns all parts, laid end to end along the dimension named above; each array names one. Nothing has to cross between parts.
All inputs are finite; a program needn't handle non-finite values.
Results may differ from the reference program's by a relative error of at most 0.0049.
Values sent between devices are 32-bit elements; how exact they have to be, the bound alone decides.
A program may use at most 128 MiB of HBM per device.

```python
import math
import jax
import jax.numpy as jnp
from jax import lax

H = 32
N = 128
P_SIZE = 64
C = 64
KH = 64
TOKENS = 4096
STRETCHES = 64
LOCAL_BITS = 4
SEQ_BITS = 2
LEVELS = 7
N_SUB = 2


def steps_of(stream_key, shape, split, smallest, high):
    loudness, own = 1.0, jax.random.fold_in(stream_key, 6)
    for axis_at, parts in split:
        draws = jnp.exp(jax.random.uniform(jax.random.fold_in(own, axis_at), (parts,), jnp.float32, smallest / len(split), high / len(split)))
        loudness = loudness * jnp.repeat(draws, shape[axis_at] // parts).reshape([-1 if axis == axis_at else 1 for axis in range(len(shape))])
    return loudness


def noise(own_key, shape, width, most, cuts=(), held_as=jnp.bfloat16):
    drawn = jax.random.normal(own_key, shape, jnp.float32) * width
    if len(cuts) > 0:
        drawn = steps_of(own_key, shape, cuts, -0.22, 0.18) * drawn
    return jnp.clip(drawn, min=-most, max=most).astype(held_as)


def setup_inputs(seed: int = 0, part: int = 0) -> dict:
    keys = jax.random.split(jax.random.key(seed), 5)
    part_keys = jax.random.split(jax.random.fold_in(keys[4], part), 5)
    query_rows = noise(part_keys[0], (H, N, TOKENS), 1.0, 6.0, ((0, 2), (1, 2), (2, 4)))
    key_rows = noise(part_keys[1], (H, N, TOKENS), N ** -0.5, 0.5, ((0, 2), (1, 2), (2, 4)))
    value_rows = noise(part_keys[2], (H, P_SIZE, TOKENS), 1.0, 6.0, ((0, 2), (2, 4)))
    level_weights = jnp.clip(jnp.exp(math.log(3.0) - 2.306499 * jax.random.uniform(part_keys[3], (H, LEVELS, TOKENS), jnp.float32) ** steps_of(part_keys[3], (H, LEVELS, TOKENS), ((0, 2), (2, 4)), -0.2, 0.2)), 0.29882812, 3.0).astype(jnp.bfloat16)
    return {"query_rows": query_rows, "key_rows": key_rows, "value_rows": value_rows, "level_weights": level_weights}


def one_head(operands):
    query_cols, key_cols, value_cols, level_part = operands
    query_part = query_cols.T
    key_part = key_cols.T
    value_part = value_cols.T
    query_f = query_part.reshape(STRETCHES, C, N).astype(jnp.float32)
    key_f = key_part.reshape(STRETCHES, C, N).astype(jnp.float32)
    value_f = value_part.reshape(STRETCHES, C, P_SIZE).astype(jnp.float32)
    weight_f = level_part.astype(jnp.float32)
    causal = jnp.tril(jnp.ones((C, C), jnp.float32)) > 0.5
    diag_weight = weight_f[0].reshape(STRETCHES, C, 1) * (C ** -0.5)
    result = jnp.zeros((STRETCHES, C, P_SIZE), jnp.float32)
    for j in range(N_SUB):
        query_block = query_f[:, :, j * KH:(j + 1) * KH]
        key_block = key_f[:, :, j * KH:(j + 1) * KH]
        scores = jnp.einsum('gtn,gsn->gts', query_block, key_block)
        scores = jnp.where(causal, scores * diag_weight, 0.0).astype(jnp.bfloat16)
        scores = lax.optimization_barrier(scores)
        result = result + jnp.einsum('gts,gsp->gtp', scores.astype(jnp.float32), value_f)
    result = result.reshape(TOKENS, P_SIZE)
    stretch_states = jnp.einsum('gsn,gsp->gnp', key_f, value_f)
    for b in range(LOCAL_BITS + SEQ_BITS):
        block_span = 2 ** b
        pairs = STRETCHES // (2 * block_span)
        sibling = stretch_states.reshape(pairs, 2, block_span, N, P_SIZE).sum(axis=2)[:, 0]
        sibling = lax.optimization_barrier(sibling.astype(jnp.bfloat16))
        upper_queries = query_part.reshape(pairs, 2, block_span * C, N)[:, 1].astype(jnp.float32)
        readout = jnp.einsum('gtn,gnp->gtp', upper_queries, sibling.astype(jnp.float32))
        factor = weight_f[b + 1].reshape(pairs, 2, block_span * C)[:, 1] * ((block_span * C) ** -0.5)
        result = result.reshape(pairs, 2, block_span * C, P_SIZE).at[:, 1].add(readout * factor[..., None])
        result = result.reshape(TOKENS, P_SIZE)
    return result.T.astype(jnp.bfloat16)


def reference(query_rows, key_rows, value_rows, level_weights):
    return lax.map(one_head, (query_rows, key_rows, value_rows, level_weights))
```

```python
import functools

import jax
import jax.numpy as jnp
from jax import lax
from jax.experimental import pallas as pl
from jax.experimental.pallas import tpu as pltpu
from jax.sharding import PartitionSpec as P

C = 64
BLOCK = 256
GROUP = 4
F32 = jnp.float32
BF16 = jnp.bfloat16
MESH = pl.DeviceIdType.MESH


def block_bits_of(tokens):
    return (tokens // BLOCK).bit_length() - 1


def local_plan(tokens):
    plan = []
    for b in range(block_bits_of(tokens)):
        for pair in range(tokens // BLOCK >> (b + 1)):
            plan.append((b, pair << (b + 1), 1 << b))
    return plan


def kernel(
    seq_size, q_hbm, k_hbm, v_hbm, w_hbm, out_hbm,
    qb, kb, vb, wb, ob, lst, own, fwd, rbuf, part, rsub,
    in_sem, w_sem, out_sem, send_sem, recv_sem, sub_send, sub_recv,
):
    heads, width, tokens = qb.shape
    groups = heads // GROUP
    blocks = tokens // BLOCK
    bits = seq_size.bit_length() - 1
    stretch_bits = (BLOCK // C).bit_length() - 1
    local_bits = (tokens // C).bit_length() - 1
    plan = local_plan(tokens)
    half = part.shape[1] // 2
    me = lax.axis_index("seq")
    sub = lax.axis_index("sub")

    def in_copy(hbm, buf, kind, g):
        heads_at = pl.ds(g * GROUP, GROUP)
        return pltpu.make_async_copy(hbm.at[heads_at], buf.at[heads_at], in_sem.at[kind, g])

    def out_copy(g):
        heads_at = pl.ds(g * GROUP, GROUP)
        return pltpu.make_async_copy(ob.at[heads_at], out_hbm.at[heads_at], out_sem.at[g])

    def state_copy(g, m, j):
        return pltpu.make_async_remote_copy(
            src_ref=fwd.at[g],
            dst_ref=rbuf.at[m, g],
            send_sem=send_sem.at[g, j],
            recv_sem=recv_sem.at[m, g],
            device_id={"seq": me + 1 + j},
            device_id_type=MESH,
        )

    def sub_copy(g):
        heads_at = pl.ds(g * GROUP, GROUP)
        return pltpu.make_async_remote_copy(
            src_ref=part.at[heads_at, pl.ds(pl.multiple_of((1 - sub) * half, half), half)],
            dst_ref=rsub.at[heads_at],
            send_sem=sub_send.at[g],
            recv_sem=sub_recv.at[g],
            device_id={"sub": 1 - sub},
            device_id_type=MESH,
        )

    barrier = pltpu.get_barrier_semaphore()
    pl.semaphore_signal(barrier, inc=1, device_id={"sub": 1 - sub}, device_id_type=MESH)
    for d in range(1, seq_size):
        pl.semaphore_signal(
            barrier, inc=1, device_id={"seq": lax.rem(me + d, seq_size)}, device_id_type=MESH
        )
    for g in range(groups):
        in_copy(k_hbm, kb, 0, g).start()
        in_copy(v_hbm, vb, 1, g).start()
    w_copy = pltpu.make_async_copy(w_hbm, wb, w_sem)
    w_copy.start()
    for g in range(groups):
        in_copy(q_hbm, qb, 2, g).start()

    lane = lax.broadcasted_iota(jnp.int32, (width, 128), 1)
    low = lane < 64
    low_f = low.astype(F32)
    low_b = low_f.astype(BF16)
    high_b = (1.0 - low_f).astype(BF16)

    def block_diag(x):
        zero = jnp.zeros((width, 128), BF16)
        rows = []
        for t in range(2):
            tile = x[:, t * 128:(t + 1) * 128]
            for mask in (low_b, high_b):
                pair = [zero, zero]
                pair[t] = tile * mask
                rows.append(jnp.concatenate(pair, axis=1))
        return jnp.concatenate(rows, axis=0)

    def states(g):
        in_copy(k_hbm, kb, 0, g).wait()
        in_copy(v_hbm, vb, 1, g).wait()
        packed = []
        for i in range(blocks):
            at = slice(i * BLOCK, (i + 1) * BLOCK)
            tiles = []
            for t in range(2):
                pair_at = pl.ds(g * GROUP + 2 * t, 2)
                values = vb[pair_at, :, at].reshape(128, BLOCK)
                keys = kb[pair_at, :, at].reshape(128, BLOCK)
                both = lax.dot_general(
                    values, keys, (((1,), (1,)), ((), ())), preferred_element_type=F32
                )
                tiles.append(jnp.where(low, both[:64], both[64:]))
            packed.append(jnp.concatenate(tiles, axis=1))
        for at, (_, first, count) in enumerate(plan):
            lst[g, at] = functools.reduce(jnp.add, packed[first:first + count]).astype(BF16)
        own[g] = functools.reduce(jnp.add, packed)

    def forward(g):
        for m in range(bits):
            @pl.when(lax.rem(me, 2 << m) == (1 << m) - 1)
            def _():
                total = own[g]
                for l in range(m):
                    state_copy(g, l, 0).wait_recv()
                    total = total + rbuf[l, g]
                fwd[g] = total
                for j in reversed(range(1 << m)):
                    state_copy(g, m, j).start()

    def forward_first(g):
        @pl.when(lax.rem(me, 2) == 0)
        def _():
            fwd[g] = own[g]
            state_copy(g, 0, 0).start()

    def forward_later(g):
        for m in range(1, bits):
            @pl.when(lax.rem(me, 2 << m) == (1 << m) - 1)
            def _():
                total = own[g]
                for l in range(m):
                    state_copy(g, l, 0).wait_recv()
                    total = total + rbuf[l, g]
                fwd[g] = total
                for j in reversed(range(1 << m)):
                    state_copy(g, m, j).start()

    def factor_row(weights, b):
        return weights[b + 1:b + 2] * (2 ** b * C) ** (-0.5)

    col = lax.broadcasted_iota(jnp.int32, (C, 128), 1)
    row = lax.broadcasted_iota(jnp.int32, (C, 128), 0)
    causal = (col >= row, col >= row + C)
    col_row = lax.broadcasted_iota(jnp.int32, (1, 128), 1) < C

    def local(g):
        in_copy(q_hbm, qb, 2, g).wait()
        for i in range(blocks):
            at = slice(i * BLOCK, (i + 1) * BLOCK)
            levels = [
                (s, b) for s, (b, first, count) in enumerate(plan)
                if i >> b & 1 and (i >> (b + 1)) << (b + 1) == first
            ]
            if levels:
                queries = qb[pl.ds(g * GROUP, GROUP), :, at].reshape(GROUP * width, BLOCK)
                lhs = jnp.concatenate([block_diag(lst[g, s]) for s, _ in levels], axis=0)
                reads = jnp.dot(lhs, queries, preferred_element_type=F32)
            for h in range(GROUP):
                head = g * GROUP + h
                weights = wb[head, :, at].astype(F32)
                scores = lax.dot_general(
                    kb[head, :, at], qb[head, :, at], (((0,), (0,)), ((), ())),
                    preferred_element_type=F32,
                )
                diag = weights[0:1] * C ** (-0.5)
                one = factor_row(weights, 0)
                two = factor_row(weights, 1)
                rows = []
                for c in range(BLOCK // C):
                    t = c // 2
                    near = slice(t * 128, (t + 1) * 128)
                    if c % 2 == 0:
                        mult = jnp.where(col_row, diag[:, near], one[:, near])
                    else:
                        mult = diag[:, near]
                    part_rows = scores[c * C:(c + 1) * C]
                    tile = jnp.where(causal[c % 2], part_rows[:, near] * mult, 0.0).astype(BF16)
                    if t == 0:
                        pair = [tile, (part_rows[:, 128:] * two[:, 128:]).astype(BF16)]
                    else:
                        pair = [jnp.zeros((C, 128), BF16), tile]
                    rows.append(jnp.concatenate(pair, axis=1))
                masked = jnp.concatenate(rows, axis=0)
                total = jnp.dot(vb[head, :, at], masked, preferred_element_type=F32)
                for n, (_, b) in enumerate(levels):
                    base = n * GROUP * 64 + h * 64
                    total = total + reads[base:base + 64] * factor_row(weights, b + stretch_bits)
                part[head, :, at] = total

    def far(g, m):
        @pl.when(lax.rem(me // (1 << m), 2) == 1)
        def _():
            waited = jnp.logical_and(
                lax.rem(me, 2 << m) == (2 << m) - 1, me != seq_size - 1
            )

            @pl.when(jnp.logical_not(waited))
            def _():
                state_copy(g, m, 0).wait_recv()

            lhs = block_diag(rbuf[m, g].astype(BF16))
            for i in range(blocks):
                at = slice(i * BLOCK, (i + 1) * BLOCK)
                queries = qb[pl.ds(g * GROUP, GROUP), :, at].reshape(GROUP * width, BLOCK)
                reads = jnp.dot(lhs, queries, preferred_element_type=F32)
                for h in range(GROUP):
                    head = g * GROUP + h
                    weights = wb[head, :, at].astype(F32)
                    part[head, :, at] += reads[h * 64:(h + 1) * 64] * factor_row(
                        weights, local_bits + m
                    )

    def finish(g):
        sub_copy(g).wait_recv()
        heads_at = pl.ds(g * GROUP, GROUP)
        mine = part[heads_at, pl.ds(pl.multiple_of(sub * half, half), half), :]
        ob[heads_at] = (mine + rsub[heads_at]).astype(BF16)
        out_copy(g).start()

    def loop(body):
        lax.fori_loop(0, groups, lambda g, carry: (body(g), carry)[1], 0)

    states(0)
    pl.semaphore_wait(barrier, seq_size)
    forward_first(0)

    @pl.loop(1, groups)
    def _(g):
        states(g)
        forward_first(g)

    w_copy.wait()

    @pl.loop(0, groups)
    def _(g):
        forward_later(g)
        local(g)

    for m in range(bits - 1):
        @pl.loop(0, groups)
        def _(g):
            far(g, m)

    @pl.loop(0, groups)
    def _(g):
        far(g, bits - 1)
        sub_copy(g).start()

        @pl.when(g > 0)
        def _():
            finish(g - 1)

    finish(groups - 1)

    @pl.loop(0, groups)
    def _(g):
        sub_copy(g).wait_send()
        out_copy(g).wait()
        for m in range(bits):
            @pl.when(lax.rem(me, 2 << m) == (1 << m) - 1)
            def _():
                for j in range(1 << m):
                    state_copy(g, m, j).wait_send()


def on_device(seq_size, query_rows, key_rows, value_rows, level_weights):
    heads, width, tokens = query_rows.shape
    value_width = value_rows.shape[1]
    groups = heads // GROUP
    bits = seq_size.bit_length() - 1
    packed = (value_width, GROUP * width)
    hbm = pl.BlockSpec(memory_space=pl.ANY)
    return pl.pallas_call(
        functools.partial(kernel, seq_size),
        out_shape=jax.ShapeDtypeStruct((heads, value_width // 2, tokens), BF16),
        in_specs=[hbm] * 4,
        out_specs=hbm,
        scratch_shapes=[
            pltpu.VMEM(query_rows.shape, BF16),
            pltpu.VMEM(key_rows.shape, BF16),
            pltpu.VMEM(value_rows.shape, BF16),
            pltpu.VMEM(level_weights.shape, BF16),
            pltpu.VMEM((heads, value_width // 2, tokens), BF16),
            pltpu.VMEM((groups, len(local_plan(tokens))) + packed, BF16),
            pltpu.VMEM((groups,) + packed, F32),
            pltpu.VMEM((groups,) + packed, F32),
            pltpu.VMEM((bits, groups) + packed, F32),
            pltpu.VMEM((heads, value_width, tokens), F32),
            pltpu.VMEM((heads, value_width // 2, tokens), F32),
            pltpu.SemaphoreType.DMA((3, groups)),
            pltpu.SemaphoreType.DMA,
            pltpu.SemaphoreType.DMA((groups,)),
            pltpu.SemaphoreType.DMA((groups, seq_size // 2)),
            pltpu.SemaphoreType.DMA((bits, groups)),
            pltpu.SemaphoreType.DMA((groups,)),
            pltpu.SemaphoreType.DMA((groups,)),
        ],
        compiler_params=pltpu.CompilerParams(
            collective_id=0, has_side_effects=True, vmem_limit_bytes=56 * 2**20
        ),
    )(query_rows, key_rows, value_rows, level_weights)


def solution(mesh):
    placed = (
        P("head", "sub", ("groups", "seq")),
        P("head", "sub", ("groups", "seq")),
        P("head", None, ("groups", "seq")),
        P("head", None, ("groups", "seq")),
    )
    return jax.shard_map(
        functools.partial(on_device, mesh.shape["seq"]),
        mesh=mesh,
        in_specs=placed,
        out_specs=P("head", "sub", ("groups", "seq")),
        check_vma=False,
    )
```

```python
import functools

import jax
import jax.numpy as jnp
from jax import lax
from jax.experimental import pallas as pl
from jax.experimental.pallas import tpu as pltpu
from jax.sharding import PartitionSpec as P

C = 64
BLOCK = 256
GROUP = 4
F32 = jnp.float32
BF16 = jnp.bfloat16
MESH = pl.DeviceIdType.MESH


def block_bits_of(tokens):
    return (tokens // BLOCK).bit_length() - 1


def local_plan(tokens):
    plan = []
    for b in range(block_bits_of(tokens)):
        for pair in range(tokens // BLOCK >> (b + 1)):
            plan.append((b, pair << (b + 1), 1 << b))
    return plan


def kernel(
    seq_size, q_hbm, k_hbm, v_hbm, w_hbm, out_hbm,
    qb, kb, vb, wb, wf, ob, lst, own, fwd, rbuf, part, rsub,
    in_sem, w_sem, out_sem, send_sem, recv_sem, sub_send, sub_recv,
):
    heads, width, tokens = qb.shape
    groups = heads // GROUP
    blocks = tokens // BLOCK
    bits = seq_size.bit_length() - 1
    stretch_bits = (BLOCK // C).bit_length() - 1
    local_bits = (tokens // C).bit_length() - 1
    plan = local_plan(tokens)
    half = part.shape[1] // 2
    me = lax.axis_index("seq")
    sub = lax.axis_index("sub")

    def in_copy(hbm, buf, kind, g):
        heads_at = pl.ds(g * GROUP, GROUP)
        return pltpu.make_async_copy(hbm.at[heads_at], buf.at[heads_at], in_sem.at[kind, g])

    def out_copy(g):
        heads_at = pl.ds(g * GROUP, GROUP)
        return pltpu.make_async_copy(ob.at[heads_at], out_hbm.at[heads_at], out_sem.at[g])

    def state_copy(g, m, j):
        return pltpu.make_async_remote_copy(
            src_ref=fwd.at[g],
            dst_ref=rbuf.at[m, g],
            send_sem=send_sem.at[g, j],
            recv_sem=recv_sem.at[m, g],
            device_id={"seq": me + 1 + j},
            device_id_type=MESH,
        )

    def sub_copy(g):
        heads_at = pl.ds(g * GROUP, GROUP)
        return pltpu.make_async_remote_copy(
            src_ref=part.at[heads_at, pl.ds(pl.multiple_of((1 - sub) * half, half), half)],
            dst_ref=rsub.at[heads_at],
            send_sem=sub_send.at[g],
            recv_sem=sub_recv.at[g],
            device_id={"sub": 1 - sub},
            device_id_type=MESH,
        )

    barrier = pltpu.get_barrier_semaphore()
    pl.semaphore_signal(barrier, inc=1, device_id={"sub": 1 - sub}, device_id_type=MESH)
    for d in range(1, seq_size):
        pl.semaphore_signal(
            barrier, inc=1, device_id={"seq": lax.rem(me + d, seq_size)}, device_id_type=MESH
        )
    for g in range(groups):
        in_copy(k_hbm, kb, 0, g).start()
        in_copy(v_hbm, vb, 1, g).start()
    w_copy = pltpu.make_async_copy(w_hbm, wb, w_sem)
    w_copy.start()
    for g in range(groups):
        in_copy(q_hbm, qb, 2, g).start()

    lane = lax.broadcasted_iota(jnp.int32, (width, 128), 1)
    low = lane < 64
    low_f = low.astype(F32)
    low_b = low_f.astype(BF16)
    high_b = (1.0 - low_f).astype(BF16)

    def block_diag(x):
        zero = jnp.zeros((width, 128), BF16)
        rows = []
        for t in range(2):
            tile = x[:, t * 128:(t + 1) * 128]
            for mask in (low_b, high_b):
                pair = [zero, zero]
                pair[t] = tile * mask
                rows.append(jnp.concatenate(pair, axis=1))
        return jnp.concatenate(rows, axis=0)

    def states(g):
        in_copy(k_hbm, kb, 0, g).wait()
        in_copy(v_hbm, vb, 1, g).wait()
        packed = []
        for i in range(blocks):
            at = slice(i * BLOCK, (i + 1) * BLOCK)
            tiles = []
            for t in range(2):
                pair_at = pl.ds(g * GROUP + 2 * t, 2)
                values = vb[pair_at, :, at].reshape(128, BLOCK)
                keys = kb[pair_at, :, at].reshape(128, BLOCK)
                both = lax.dot_general(
                    values, keys, (((1,), (1,)), ((), ())), preferred_element_type=F32
                )
                tiles.append(jnp.where(low, both[:64], both[64:]))
            packed.append(jnp.concatenate(tiles, axis=1))
        for at, (_, first, count) in enumerate(plan):
            lst[g, at] = functools.reduce(jnp.add, packed[first:first + count]).astype(BF16)
        own[g] = functools.reduce(jnp.add, packed)

    def forward_first(g):
        @pl.when(lax.rem(me, 2) == 0)
        def _():
            fwd[g] = own[g]
            state_copy(g, 0, 0).start()

    def forward_later(g):
        for m in range(1, bits):
            @pl.when(lax.rem(me, 2 << m) == (1 << m) - 1)
            def _():
                total = own[g]
                for l in range(m):
                    state_copy(g, l, 0).wait_recv()
                    total = total + rbuf[l, g]
                fwd[g] = total
                for j in reversed(range(1 << m)):
                    state_copy(g, m, j).start()

    def factor_row(head, level, at):
        return wf[level, pl.ds(head, 1), at]

    col = lax.broadcasted_iota(jnp.int32, (C, 128), 1)
    row = lax.broadcasted_iota(jnp.int32, (C, 128), 0)
    causal = (col >= row, col >= row + C)
    col_row = lax.broadcasted_iota(jnp.int32, (1, 128), 1) < C

    def local(g):
        in_copy(q_hbm, qb, 2, g).wait()
        for i in range(blocks):
            at = slice(i * BLOCK, (i + 1) * BLOCK)
            levels = [
                (s, b) for s, (b, first, count) in enumerate(plan)
                if i >> b & 1 and (i >> (b + 1)) << (b + 1) == first
            ]
            if levels:
                queries = qb[pl.ds(g * GROUP, GROUP), :, at].reshape(GROUP * width, BLOCK)
                lhs = jnp.concatenate([block_diag(lst[g, s]) for s, _ in levels], axis=0)
                reads = jnp.dot(lhs, queries, preferred_element_type=F32)
            for h in range(GROUP):
                head = g * GROUP + h
                scores = lax.dot_general(
                    kb[head, :, at], qb[head, :, at], (((0,), (0,)), ((), ())),
                    preferred_element_type=F32,
                )
                diag, one, two = (factor_row(head, n, at) for n in range(3))
                rows = []
                for c in range(BLOCK // C):
                    t = c // 2
                    near = slice(t * 128, (t + 1) * 128)
                    if c % 2 == 0:
                        mult = jnp.where(col_row, diag[:, near], one[:, near])
                    else:
                        mult = diag[:, near]
                    part_rows = scores[c * C:(c + 1) * C]
                    tile = jnp.where(causal[c % 2], part_rows[:, near] * mult, 0.0).astype(BF16)
                    if t == 0:
                        pair = [tile, (part_rows[:, 128:] * two[:, 128:]).astype(BF16)]
                    else:
                        pair = [jnp.zeros((C, 128), BF16), tile]
                    rows.append(jnp.concatenate(pair, axis=1))
                masked = jnp.concatenate(rows, axis=0)
                total = jnp.dot(vb[head, :, at], masked, preferred_element_type=F32)
                for n, (_, b) in enumerate(levels):
                    base = n * GROUP * 64 + h * 64
                    total = total + reads[base:base + 64] * factor_row(
                        head, b + stretch_bits + 1, at
                    )
                part[head, :, at] = total

    def far(g, m):
        @pl.when(lax.rem(me // (1 << m), 2) == 1)
        def _():
            waited = jnp.logical_and(
                lax.rem(me, 2 << m) == (2 << m) - 1, me != seq_size - 1
            )

            @pl.when(jnp.logical_not(waited))
            def _():
                state_copy(g, m, 0).wait_recv()

            lhs = block_diag(rbuf[m, g].astype(BF16))
            for i in range(blocks):
                at = slice(i * BLOCK, (i + 1) * BLOCK)
                queries = qb[pl.ds(g * GROUP, GROUP), :, at].reshape(GROUP * width, BLOCK)
                reads = jnp.dot(lhs, queries, preferred_element_type=F32)
                for h in range(GROUP):
                    head = g * GROUP + h
                    part[head, :, at] += reads[h * 64:(h + 1) * 64] * factor_row(
                        head, local_bits + m + 1, at
                    )

    def finish(g):
        sub_copy(g).wait_recv()
        heads_at = pl.ds(g * GROUP, GROUP)
        mine = part[heads_at, pl.ds(pl.multiple_of(sub * half, half), half), :]
        ob[heads_at] = (mine + rsub[heads_at]).astype(BF16)
        out_copy(g).start()

    def loop(body):
        lax.fori_loop(0, groups, lambda g, carry: (body(g), carry)[1], 0)

    states(0)
    pl.semaphore_wait(barrier, seq_size)
    forward_first(0)

    @pl.loop(1, groups)
    def _(g):
        states(g)
        forward_first(g)

    w_copy.wait()
    wf[0] = wb[0].astype(F32) * C ** (-0.5)
    for b in range(local_bits + bits):
        wf[b + 1] = wb[b + 1].astype(F32) * (2 ** b * C) ** (-0.5)

    def send(g):
        for m in range(bits):
            far(g, m)
        sub_copy(g).start()

    @pl.loop(0, groups)
    def _(g):
        local(g)
        forward_later(g)

        @pl.when(g > 0)
        def _():
            send(g - 1)

        @pl.when(g > 1)
        def _():
            finish(g - 2)

    send(groups - 1)
    if groups > 1:
        finish(groups - 2)
    finish(groups - 1)

    @pl.loop(0, groups)
    def _(g):
        sub_copy(g).wait_send()
        out_copy(g).wait()
        for m in range(bits):
            @pl.when(lax.rem(me, 2 << m) == (1 << m) - 1)
            def _():
                for j in range(1 << m):
                    state_copy(g, m, j).wait_send()


def on_device(seq_size, query_rows, key_rows, value_rows, level_weights):
    heads, width, tokens = query_rows.shape
    value_width = value_rows.shape[1]
    weights = jnp.swapaxes(level_weights, 0, 1)
    groups = heads // GROUP
    bits = seq_size.bit_length() - 1
    packed = (value_width, GROUP * width)
    hbm = pl.BlockSpec(memory_space=pltpu.HBM)
    return pl.pallas_call(
        functools.partial(kernel, seq_size),
        out_shape=jax.ShapeDtypeStruct((heads, value_width // 2, tokens), BF16),
        in_specs=[hbm] * 4,
        out_specs=hbm,
        scratch_shapes=[
            pltpu.VMEM(query_rows.shape, BF16),
            pltpu.VMEM(key_rows.shape, BF16),
            pltpu.VMEM(value_rows.shape, BF16),
            pltpu.VMEM(weights.shape, BF16),
            pltpu.VMEM(weights.shape, F32),
            pltpu.VMEM((heads, value_width // 2, tokens), BF16),
            pltpu.VMEM((groups, len(local_plan(tokens))) + packed, BF16),
            pltpu.VMEM((groups,) + packed, F32),
            pltpu.VMEM((groups,) + packed, F32),
            pltpu.VMEM((bits, groups) + packed, F32),
            pltpu.VMEM((heads, value_width, tokens), F32),
            pltpu.VMEM((heads, value_width // 2, tokens), F32),
            pltpu.SemaphoreType.DMA((3, groups)),
            pltpu.SemaphoreType.DMA,
            pltpu.SemaphoreType.DMA((groups,)),
            pltpu.SemaphoreType.DMA((groups, seq_size // 2)),
            pltpu.SemaphoreType.DMA((bits, groups)),
            pltpu.SemaphoreType.DMA((groups,)),
            pltpu.SemaphoreType.DMA((groups,)),
        ],
        compiler_params=pltpu.CompilerParams(
            collective_id=0, has_side_effects=True, vmem_limit_bytes=56 * 2**20
        ),
    )(query_rows, key_rows, value_rows, weights)


def solution(mesh):
    placed = (
        P("head", "sub", ("groups", "seq")),
        P("head", "sub", ("groups", "seq")),
        P("head", None, ("groups", "seq")),
        P("head", None, ("groups", "seq")),
    )
    return jax.shard_map(
        functools.partial(on_device, mesh.shape["seq"]),
        mesh=mesh,
        in_specs=placed,
        out_specs=P("head", "sub", ("groups", "seq")),
        check_vma=False,
    )
```

```python
import functools

import jax
import jax.numpy as jnp
from jax import lax
from jax.experimental import pallas as pl
from jax.experimental.pallas import tpu as pltpu
from jax.sharding import PartitionSpec as P

C = 64
BLOCK = 256
GROUP = 4
F32 = jnp.float32
BF16 = jnp.bfloat16
MESH = pl.DeviceIdType.MESH


def block_bits_of(tokens):
    return (tokens // BLOCK).bit_length() - 1


def local_plan(tokens):
    plan = []
    for b in range(block_bits_of(tokens)):
        for pair in range(tokens // BLOCK >> (b + 1)):
            plan.append((b, pair << (b + 1), 1 << b))
    return plan


def kernel(
    seq_size, q_hbm, k_hbm, v_hbm, w_hbm, out_hbm,
    qb, kb, vb, wb, wf, ob, lst, own, fwd, rbuf, part, rsub,
    in_sem, w_sem, out_sem, send_sem, recv_sem, sub_send, sub_recv,
):
    heads, width, tokens = qb.shape
    groups = heads // GROUP
    blocks = tokens // BLOCK
    bits = seq_size.bit_length() - 1
    stretch_bits = (BLOCK // C).bit_length() - 1
    local_bits = (tokens // C).bit_length() - 1
    plan = local_plan(tokens)
    half = part.shape[1] // 2
    me = lax.axis_index("seq")
    sub = lax.axis_index("sub")

    def in_copy(hbm, buf, kind, g):
        heads_at = pl.ds(g * GROUP, GROUP)
        return pltpu.make_async_copy(hbm.at[heads_at], buf.at[heads_at], in_sem.at[kind, g])

    def out_copy(g):
        heads_at = pl.ds(g * GROUP, GROUP)
        return pltpu.make_async_copy(ob.at[heads_at], out_hbm.at[heads_at], out_sem.at[g])

    def state_copy(g, m, j):
        return pltpu.make_async_remote_copy(
            src_ref=fwd.at[g],
            dst_ref=rbuf.at[m, g],
            send_sem=send_sem.at[g, j],
            recv_sem=recv_sem.at[m, g],
            device_id={"seq": me + 1 + j},
            device_id_type=MESH,
        )

    def sub_copy(g):
        heads_at = pl.ds(g * GROUP, GROUP)
        return pltpu.make_async_remote_copy(
            src_ref=part.at[heads_at, pl.ds(pl.multiple_of((1 - sub) * half, half), half)],
            dst_ref=rsub.at[heads_at],
            send_sem=sub_send.at[g],
            recv_sem=sub_recv.at[g],
            device_id={"sub": 1 - sub},
            device_id_type=MESH,
        )

    barrier = pltpu.get_barrier_semaphore()
    pl.semaphore_signal(barrier, inc=1, device_id={"sub": 1 - sub}, device_id_type=MESH)
    for d in range(1, seq_size):
        pl.semaphore_signal(
            barrier, inc=1, device_id={"seq": lax.rem(me + d, seq_size)}, device_id_type=MESH
        )
    for g in range(groups):
        in_copy(k_hbm, kb, 0, g).start()
        in_copy(v_hbm, vb, 1, g).start()
    w_copy = pltpu.make_async_copy(w_hbm, wb, w_sem)
    w_copy.start()
    for g in range(groups):
        in_copy(q_hbm, qb, 2, g).start()

    lane = lax.broadcasted_iota(jnp.int32, (width, 128), 1)
    low = lane < 64
    low_f = low.astype(F32)
    low_b = low_f.astype(BF16)
    high_b = (1.0 - low_f).astype(BF16)

    def block_diag(x):
        zero = jnp.zeros((width, 128), BF16)
        rows = []
        for t in range(2):
            tile = x[:, t * 128:(t + 1) * 128]
            for mask in (low_b, high_b):
                pair = [zero, zero]
                pair[t] = tile * mask
                rows.append(jnp.concatenate(pair, axis=1))
        return jnp.concatenate(rows, axis=0)

    def states(g):
        in_copy(k_hbm, kb, 0, g).wait()
        in_copy(v_hbm, vb, 1, g).wait()
        packed = []
        for i in range(blocks):
            at = slice(i * BLOCK, (i + 1) * BLOCK)
            tiles = []
            for t in range(2):
                pair_at = pl.ds(g * GROUP + 2 * t, 2)
                values = vb[pair_at, :, at].reshape(128, BLOCK)
                keys = kb[pair_at, :, at].reshape(128, BLOCK)
                both = lax.dot_general(
                    values, keys, (((1,), (1,)), ((), ())), preferred_element_type=F32
                )
                tiles.append(jnp.where(low, both[:64], both[64:]))
            packed.append(jnp.concatenate(tiles, axis=1))
        for at, (_, first, count) in enumerate(plan):
            lst[g, at] = functools.reduce(jnp.add, packed[first:first + count]).astype(BF16)
        own[g] = functools.reduce(jnp.add, packed)

    def forward_first(g):
        @pl.when(lax.rem(me, 2) == 0)
        def _():
            fwd[g] = own[g]
            state_copy(g, 0, 0).start()

    def forward_later(g):
        for m in range(1, bits):
            @pl.when(lax.rem(me, 2 << m) == (1 << m) - 1)
            def _():
                total = own[g]
                for l in range(m):
                    state_copy(g, l, 0).wait_recv()
                    total = total + rbuf[l, g]
                fwd[g] = total
                for j in reversed(range(1 << m)):
                    state_copy(g, m, j).start()

    def factor_row(head, level, at):
        return wf[level, pl.ds(head, 1), at]

    col = lax.broadcasted_iota(jnp.int32, (C, 128), 1)
    row = lax.broadcasted_iota(jnp.int32, (C, 128), 0)
    causal = (col >= row, col >= row + C)
    col_row = lax.broadcasted_iota(jnp.int32, (1, 128), 1) < C

    def local(g):
        in_copy(q_hbm, qb, 2, g).wait()
        for i in range(blocks):
            at = slice(i * BLOCK, (i + 1) * BLOCK)
            levels = [
                (s, b) for s, (b, first, count) in enumerate(plan)
                if i >> b & 1 and (i >> (b + 1)) << (b + 1) == first
            ]
            if levels:
                queries = qb[pl.ds(g * GROUP, GROUP), :, at].reshape(GROUP * width, BLOCK)
                lhs = jnp.concatenate([block_diag(lst[g, s]) for s, _ in levels], axis=0)
                reads = jnp.dot(lhs, queries, preferred_element_type=F32)
            grid = []
            for h in range(GROUP):
                head = g * GROUP + h
                scores = lax.dot_general(
                    kb[head, :, at], qb[head, :, at], (((0,), (0,)), ((), ())),
                    preferred_element_type=F32,
                )
                diag, one, two = (factor_row(head, n, at) for n in range(3))
                rows = []
                for c in range(BLOCK // C):
                    t = c // 2
                    near = slice(t * 128, (t + 1) * 128)
                    if c % 2 == 0:
                        mult = jnp.where(col_row, diag[:, near], one[:, near])
                    else:
                        mult = diag[:, near]
                    part_rows = scores[c * C:(c + 1) * C]
                    tile = jnp.where(causal[c % 2], part_rows[:, near] * mult, 0.0).astype(BF16)
                    if t == 0:
                        pair = [tile, (part_rows[:, 128:] * two[:, 128:]).astype(BF16)]
                    else:
                        pair = [jnp.zeros((C, 128), BF16), tile]
                    rows.append(jnp.concatenate(pair, axis=1))
                grid.append(jnp.concatenate(rows, axis=0))
            for h in range(GROUP):
                head = g * GROUP + h
                total = jnp.dot(vb[head, :, at], grid[h], preferred_element_type=F32)
                for n, (_, b) in enumerate(levels):
                    base = n * GROUP * 64 + h * 64
                    total = total + reads[base:base + 64] * factor_row(
                        head, b + stretch_bits + 1, at
                    )
                part[head, :, at] = total

    def far(g, m):
        @pl.when(lax.rem(me // (1 << m), 2) == 1)
        def _():
            waited = jnp.logical_and(
                lax.rem(me, 2 << m) == (2 << m) - 1, me != seq_size - 1
            )

            @pl.when(jnp.logical_not(waited))
            def _():
                state_copy(g, m, 0).wait_recv()

            lhs = block_diag(rbuf[m, g].astype(BF16))
            for i in range(blocks):
                at = slice(i * BLOCK, (i + 1) * BLOCK)
                queries = qb[pl.ds(g * GROUP, GROUP), :, at].reshape(GROUP * width, BLOCK)
                reads = jnp.dot(lhs, queries, preferred_element_type=F32)
                for h in range(GROUP):
                    head = g * GROUP + h
                    part[head, :, at] += reads[h * 64:(h + 1) * 64] * factor_row(
                        head, local_bits + m + 1, at
                    )

    def finish(g):
        sub_copy(g).wait_recv()
        heads_at = pl.ds(g * GROUP, GROUP)
        mine = part[heads_at, pl.ds(pl.multiple_of(sub * half, half), half), :]
        ob[heads_at] = (mine + rsub[heads_at]).astype(BF16)
        out_copy(g).start()

    def loop(body):
        lax.fori_loop(0, groups, lambda g, carry: (body(g), carry)[1], 0)

    states(0)
    pl.semaphore_wait(barrier, seq_size)
    forward_first(0)

    @pl.loop(1, groups)
    def _(g):
        states(g)
        forward_first(g)

    w_copy.wait()
    wf[0] = wb[0].astype(F32) * C ** (-0.5)
    for b in range(local_bits + bits):
        wf[b + 1] = wb[b + 1].astype(F32) * (2 ** b * C) ** (-0.5)

    def send(g):
        for m in range(bits):
            far(g, m)
        sub_copy(g).start()

    @pl.loop(0, groups)
    def _(g):
        local(g)
        forward_later(g)

        @pl.when(g > 0)
        def _():
            send(g - 1)

        @pl.when(g > 1)
        def _():
            finish(g - 2)

    send(groups - 1)
    if groups > 1:
        finish(groups - 2)
    finish(groups - 1)

    @pl.loop(0, groups)
    def _(g):
        sub_copy(g).wait_send()
        out_copy(g).wait()
        for m in range(bits):
            @pl.when(lax.rem(me, 2 << m) == (1 << m) - 1)
            def _():
                for j in range(1 << m):
                    state_copy(g, m, j).wait_send()


def on_device(seq_size, query_rows, key_rows, value_rows, level_weights):
    heads, width, tokens = query_rows.shape
    value_width = value_rows.shape[1]
    weights = jnp.swapaxes(level_weights, 0, 1)
    groups = heads // GROUP
    bits = seq_size.bit_length() - 1
    packed = (value_width, GROUP * width)
    hbm = pl.BlockSpec(memory_space=pltpu.HBM)
    return pl.pallas_call(
        functools.partial(kernel, seq_size),
        out_shape=jax.ShapeDtypeStruct((heads, value_width // 2, tokens), BF16),
        in_specs=[hbm] * 4,
        out_specs=hbm,
        scratch_shapes=[
            pltpu.VMEM(query_rows.shape, BF16),
            pltpu.VMEM(key_rows.shape, BF16),
            pltpu.VMEM(value_rows.shape, BF16),
            pltpu.VMEM(weights.shape, BF16),
            pltpu.VMEM(weights.shape, F32),
            pltpu.VMEM((heads, value_width // 2, tokens), BF16),
            pltpu.VMEM((groups, len(local_plan(tokens))) + packed, BF16),
            pltpu.VMEM((groups,) + packed, F32),
            pltpu.VMEM((groups,) + packed, F32),
            pltpu.VMEM((bits, groups) + packed, F32),
            pltpu.VMEM((heads, value_width, tokens), F32),
            pltpu.VMEM((heads, value_width // 2, tokens), F32),
            pltpu.SemaphoreType.DMA((3, groups)),
            pltpu.SemaphoreType.DMA,
            pltpu.SemaphoreType.DMA((groups,)),
            pltpu.SemaphoreType.DMA((groups, seq_size // 2)),
            pltpu.SemaphoreType.DMA((bits, groups)),
            pltpu.SemaphoreType.DMA((groups,)),
            pltpu.SemaphoreType.DMA((groups,)),
        ],
        compiler_params=pltpu.CompilerParams(
            collective_id=0, has_side_effects=True, vmem_limit_bytes=56 * 2**20
        ),
    )(query_rows, key_rows, value_rows, weights)


def solution(mesh):
    placed = (
        P("head", "sub", ("groups", "seq")),
        P("head", "sub", ("groups", "seq")),
        P("head", None, ("groups", "seq")),
        P("head", None, ("groups", "seq")),
    )
    return jax.shard_map(
        functools.partial(on_device, mesh.shape["seq"]),
        mesh=mesh,
        in_specs=placed,
        out_specs=P("head", "sub", ("groups", "seq")),
        check_vma=False,
    )
```

```python
import functools

import jax
import jax.numpy as jnp
from jax import lax
from jax.experimental import pallas as pl
from jax.experimental.pallas import tpu as pltpu
from jax.sharding import PartitionSpec as P

C = 64
BLOCK = 256
GROUP = 4
F32 = jnp.float32
BF16 = jnp.bfloat16
MESH = pl.DeviceIdType.MESH


def block_bits_of(tokens):
    return (tokens // BLOCK).bit_length() - 1


def local_plan(tokens):
    plan = []
    for b in range(block_bits_of(tokens)):
        for pair in range(tokens // BLOCK >> (b + 1)):
            plan.append((b, pair << (b + 1), 1 << b))
    return plan


def kernel(
    seq_size, q_hbm, k_hbm, v_hbm, w_hbm, out_hbm,
    qb, kb, vb, wb, wf, ob, lst, own, fwd, rbuf, part, rsub,
    in_sem, w_sem, out_sem, send_sem, recv_sem, sub_send, sub_recv,
):
    heads, width, tokens = qb.shape
    groups = heads // GROUP
    blocks = tokens // BLOCK
    bits = seq_size.bit_length() - 1
    stretch_bits = (BLOCK // C).bit_length() - 1
    local_bits = (tokens // C).bit_length() - 1
    plan = local_plan(tokens)
    half = part.shape[1] // 2
    me = lax.axis_index("seq")
    sub = lax.axis_index("sub")

    def in_copy(hbm, buf, kind, g):
        heads_at = pl.ds(g * GROUP, GROUP)
        return pltpu.make_async_copy(hbm.at[heads_at], buf.at[heads_at], in_sem.at[kind, g])

    def out_copy(g):
        heads_at = pl.ds(g * GROUP, GROUP)
        return pltpu.make_async_copy(ob.at[heads_at], out_hbm.at[heads_at], out_sem.at[g])

    def state_copy(g, m, j):
        return pltpu.make_async_remote_copy(
            src_ref=fwd.at[g],
            dst_ref=rbuf.at[m, g],
            send_sem=send_sem.at[g, j],
            recv_sem=recv_sem.at[m, g],
            device_id={"seq": me + 1 + j},
            device_id_type=MESH,
        )

    def sub_copy(g):
        heads_at = pl.ds(g * GROUP, GROUP)
        return pltpu.make_async_remote_copy(
            src_ref=part.at[heads_at, pl.ds(pl.multiple_of((1 - sub) * half, half), half)],
            dst_ref=rsub.at[heads_at],
            send_sem=sub_send.at[g],
            recv_sem=sub_recv.at[g],
            device_id={"sub": 1 - sub},
            device_id_type=MESH,
        )

    barrier = pltpu.get_barrier_semaphore()
    pl.semaphore_signal(barrier, inc=1, device_id={"sub": 1 - sub}, device_id_type=MESH)
    for d in range(1, seq_size):
        pl.semaphore_signal(
            barrier, inc=1, device_id={"seq": lax.rem(me + d, seq_size)}, device_id_type=MESH
        )
    for g in range(groups):
        in_copy(k_hbm, kb, 0, g).start()
        in_copy(v_hbm, vb, 1, g).start()
    w_copy = pltpu.make_async_copy(w_hbm, wb, w_sem)
    w_copy.start()
    for g in range(groups):
        in_copy(q_hbm, qb, 2, g).start()

    lane = lax.broadcasted_iota(jnp.int32, (width, 128), 1)
    low = lane < 64
    low_f = low.astype(F32)
    low_b = low_f.astype(BF16)
    high_b = (1.0 - low_f).astype(BF16)

    def block_diag(x):
        zero = jnp.zeros((width, 128), BF16)
        rows = []
        for t in range(2):
            tile = x[:, t * 128:(t + 1) * 128]
            for mask in (low_b, high_b):
                pair = [zero, zero]
                pair[t] = tile * mask
                rows.append(jnp.concatenate(pair, axis=1))
        return jnp.concatenate(rows, axis=0)

    def states(g):
        in_copy(k_hbm, kb, 0, g).wait()
        in_copy(v_hbm, vb, 1, g).wait()
        packed = []
        for i in range(blocks):
            at = slice(i * BLOCK, (i + 1) * BLOCK)
            tiles = []
            for t in range(2):
                pair_at = pl.ds(g * GROUP + 2 * t, 2)
                values = vb[pair_at, :, at].reshape(128, BLOCK)
                keys = kb[pair_at, :, at].reshape(128, BLOCK)
                both = lax.dot_general(
                    values, keys, (((1,), (1,)), ((), ())), preferred_element_type=F32
                )
                tiles.append(jnp.where(low, both[:64], both[64:]))
            packed.append(jnp.concatenate(tiles, axis=1))
        for at, (_, first, count) in enumerate(plan):
            lst[g, at] = functools.reduce(jnp.add, packed[first:first + count]).astype(BF16)
        own[g] = functools.reduce(jnp.add, packed)

    def forward_first(g):
        @pl.when(lax.rem(me, 2) == 0)
        def _():
            fwd[g] = own[g]
            state_copy(g, 0, 0).start()

    def forward_later(g):
        for m in range(1, bits):
            @pl.when(lax.rem(me, 2 << m) == (1 << m) - 1)
            def _():
                total = own[g]
                for l in range(m):
                    state_copy(g, l, 0).wait_recv()
                    total = total + rbuf[l, g]
                fwd[g] = total
                for j in reversed(range(1 << m)):
                    state_copy(g, m, j).start()

    def factor_row(head, level, at):
        return wf[level, pl.ds(head, 1), at]

    col = lax.broadcasted_iota(jnp.int32, (C, 128), 1)
    row = lax.broadcasted_iota(jnp.int32, (C, 128), 0)
    causal = (col >= row, col >= row + C)
    col_row = lax.broadcasted_iota(jnp.int32, (1, 128), 1) < C

    def local(g):
        in_copy(q_hbm, qb, 2, g).wait()
        for i in range(blocks):
            at = slice(i * BLOCK, (i + 1) * BLOCK)
            levels = [
                (s, b) for s, (b, first, count) in enumerate(plan)
                if i >> b & 1 and (i >> (b + 1)) << (b + 1) == first
            ]
            if levels:
                queries = qb[pl.ds(g * GROUP, GROUP), :, at].reshape(GROUP * width, BLOCK)
                lhs = jnp.concatenate([block_diag(lst[g, s]) for s, _ in levels], axis=0)
                reads = jnp.dot(lhs, queries, preferred_element_type=F32)
            grid = []
            for h in range(GROUP):
                head = g * GROUP + h
                scores = lax.dot_general(
                    kb[head, :, at], qb[head, :, at], (((0,), (0,)), ((), ())),
                    preferred_element_type=F32,
                )
                diag, one, two = (factor_row(head, n, at) for n in range(3))
                rows = []
                for c in range(BLOCK // C):
                    t = c // 2
                    near = slice(t * 128, (t + 1) * 128)
                    if c % 2 == 0:
                        mult = jnp.where(col_row, diag[:, near], one[:, near])
                    else:
                        mult = diag[:, near]
                    part_rows = scores[c * C:(c + 1) * C]
                    tile = jnp.where(causal[c % 2], part_rows[:, near] * mult, 0.0).astype(BF16)
                    if t == 0:
                        pair = [tile, (part_rows[:, 128:] * two[:, 128:]).astype(BF16)]
                    else:
                        pair = [jnp.zeros((C, 128), BF16), tile]
                    rows.append(jnp.concatenate(pair, axis=1))
                grid.append(jnp.concatenate(rows, axis=0))
            for h in range(GROUP):
                head = g * GROUP + h
                total = jnp.dot(vb[head, :, at], grid[h], preferred_element_type=F32)
                for n, (_, b) in enumerate(levels):
                    base = n * GROUP * 64 + h * 64
                    total = total + reads[base:base + 64] * factor_row(
                        head, b + stretch_bits + 1, at
                    )
                part[head, :, at] = total

    def far(g, m):
        @pl.when(lax.rem(me // (1 << m), 2) == 1)
        def _():
            waited = jnp.logical_and(
                lax.rem(me, 2 << m) == (2 << m) - 1, me != seq_size - 1
            )

            @pl.when(jnp.logical_not(waited))
            def _():
                state_copy(g, m, 0).wait_recv()

            lhs = block_diag(rbuf[m, g].astype(BF16))
            for i in range(blocks):
                at = slice(i * BLOCK, (i + 1) * BLOCK)
                queries = qb[pl.ds(g * GROUP, GROUP), :, at].reshape(GROUP * width, BLOCK)
                reads = jnp.dot(lhs, queries, preferred_element_type=F32)
                for h in range(GROUP):
                    head = g * GROUP + h
                    part[head, :, at] += reads[h * 64:(h + 1) * 64] * factor_row(
                        head, local_bits + m + 1, at
                    )

    def finish(g):
        sub_copy(g).wait_recv()
        heads_at = pl.ds(g * GROUP, GROUP)
        mine = part[heads_at, pl.ds(pl.multiple_of(sub * half, half), half), :]
        ob[heads_at] = (mine + rsub[heads_at]).astype(BF16)
        out_copy(g).start()

    def loop(body):
        lax.fori_loop(0, groups, lambda g, carry: (body(g), carry)[1], 0)

    states(0)
    pl.semaphore_wait(barrier, seq_size)
    forward_first(0)

    @pl.loop(1, groups)
    def _(g):
        states(g)
        forward_first(g)

    w_copy.wait()
    wf[0] = wb[0].astype(F32) * C ** (-0.5)
    for b in range(local_bits + bits):
        wf[b + 1] = wb[b + 1].astype(F32) * (2 ** b * C) ** (-0.5)

    def send(g):
        for m in range(bits):
            far(g, m)
        sub_copy(g).start()

    @pl.loop(0, groups)
    def _(g):
        local(g)
        forward_later(g)

        @pl.when(g > 0)
        def _():
            send(g - 1)

        @pl.when(g > 1)
        def _():
            finish(g - 2)

    send(groups - 1)
    if groups > 1:
        finish(groups - 2)
    finish(groups - 1)

    @pl.loop(0, groups)
    def _(g):
        sub_copy(g).wait_send()
        out_copy(g).wait()
        for m in range(bits):
            @pl.when(lax.rem(me, 2 << m) == (1 << m) - 1)
            def _():
                for j in range(1 << m):
                    state_copy(g, m, j).wait_send()


def on_device(seq_size, query_rows, key_rows, value_rows, level_weights):
    heads, width, tokens = query_rows.shape
    value_width = value_rows.shape[1]
    weights = jnp.swapaxes(level_weights, 0, 1)
    groups = heads // GROUP
    bits = seq_size.bit_length() - 1
    packed = (value_width, GROUP * width)
    hbm = pl.BlockSpec(memory_space=pltpu.HBM)
    return pl.pallas_call(
        functools.partial(kernel, seq_size),
        out_shape=jax.ShapeDtypeStruct((heads, value_width // 2, tokens), BF16),
        in_specs=[hbm] * 4,
        out_specs=pl.BlockSpec(memory_space=pl.ANY),
        scratch_shapes=[
            pltpu.VMEM(query_rows.shape, BF16),
            pltpu.VMEM(key_rows.shape, BF16),
            pltpu.VMEM(value_rows.shape, BF16),
            pltpu.VMEM(weights.shape, BF16),
            pltpu.VMEM(weights.shape, F32),
            pltpu.VMEM((heads, value_width // 2, tokens), BF16),
            pltpu.VMEM((groups, len(local_plan(tokens))) + packed, BF16),
            pltpu.VMEM((groups,) + packed, F32),
            pltpu.VMEM((groups,) + packed, F32),
            pltpu.VMEM((bits, groups) + packed, F32),
            pltpu.VMEM((heads, value_width, tokens), F32),
            pltpu.VMEM((heads, value_width // 2, tokens), F32),
            pltpu.SemaphoreType.DMA((3, groups)),
            pltpu.SemaphoreType.DMA,
            pltpu.SemaphoreType.DMA((groups,)),
            pltpu.SemaphoreType.DMA((groups, seq_size // 2)),
            pltpu.SemaphoreType.DMA((bits, groups)),
            pltpu.SemaphoreType.DMA((groups,)),
            pltpu.SemaphoreType.DMA((groups,)),
        ],
        compiler_params=pltpu.CompilerParams(
            collective_id=0, has_side_effects=True, vmem_limit_bytes=52 * 2**20
        ),
    )(query_rows, key_rows, value_rows, weights)


def solution(mesh):
    placed = (
        P("head", "sub", ("groups", "seq")),
        P("head", "sub", ("groups", "seq")),
        P("head", None, ("groups", "seq")),
        P("head", None, ("groups", "seq")),
    )
    return jax.shard_map(
        functools.partial(on_device, mesh.shape["seq"]),
        mesh=mesh,
        in_specs=placed,
        out_specs=P("head", "sub", ("groups", "seq")),
        check_vma=False,
    )
```

```python
import functools

import jax
import jax.numpy as jnp
from jax import lax
from jax.experimental import pallas as pl
from jax.experimental.pallas import tpu as pltpu
from jax.sharding import PartitionSpec as P

C = 64
BLOCK = 256
GROUP = 4
F32 = jnp.float32
BF16 = jnp.bfloat16
MESH = pl.DeviceIdType.MESH


def block_bits_of(tokens):
    return (tokens // BLOCK).bit_length() - 1


def local_plan(tokens):
    plan = []
    for b in range(block_bits_of(tokens)):
        for pair in range(tokens // BLOCK >> (b + 1)):
            plan.append((b, pair << (b + 1), 1 << b))
    return plan


def kernel(
    seq_size, q_hbm, k_hbm, v_hbm, w_hbm, out,
    qb, kb, vb, wb, wf, lst, own, fwd, rbuf, part, rsub,
    in_sem, w_sem, send_sem, recv_sem, sub_send, sub_recv,
):
    heads, width, tokens = qb.shape
    groups = heads // GROUP
    blocks = tokens // BLOCK
    bits = seq_size.bit_length() - 1
    stretch_bits = (BLOCK // C).bit_length() - 1
    local_bits = (tokens // C).bit_length() - 1
    plan = local_plan(tokens)
    half = part.shape[1] // 2
    me = lax.axis_index("seq")
    sub = lax.axis_index("sub")

    def in_copy(hbm, buf, kind, g):
        heads_at = pl.ds(g * GROUP, GROUP)
        return pltpu.make_async_copy(hbm.at[heads_at], buf.at[heads_at], in_sem.at[kind, g])

    def state_copy(g, m, j):
        return pltpu.make_async_remote_copy(
            src_ref=fwd.at[g],
            dst_ref=rbuf.at[m, g],
            send_sem=send_sem.at[g, j],
            recv_sem=recv_sem.at[m, g],
            device_id={"seq": me + 1 + j},
            device_id_type=MESH,
        )

    def sub_copy(g):
        heads_at = pl.ds(g * GROUP, GROUP)
        return pltpu.make_async_remote_copy(
            src_ref=part.at[heads_at, pl.ds(pl.multiple_of((1 - sub) * half, half), half)],
            dst_ref=rsub.at[heads_at],
            send_sem=sub_send.at[g],
            recv_sem=sub_recv.at[g],
            device_id={"sub": 1 - sub},
            device_id_type=MESH,
        )

    barrier = pltpu.get_barrier_semaphore()
    pl.semaphore_signal(barrier, inc=1, device_id={"sub": 1 - sub}, device_id_type=MESH)
    for d in range(1, seq_size):
        pl.semaphore_signal(
            barrier, inc=1, device_id={"seq": lax.rem(me + d, seq_size)}, device_id_type=MESH
        )
    for g in range(groups):
        in_copy(k_hbm, kb, 0, g).start()
        in_copy(v_hbm, vb, 1, g).start()
    w_copy = pltpu.make_async_copy(w_hbm, wb, w_sem)
    w_copy.start()
    for g in range(groups):
        in_copy(q_hbm, qb, 2, g).start()

    lane = lax.broadcasted_iota(jnp.int32, (width, 128), 1)
    low = lane < 64
    low_f = low.astype(F32)
    low_b = low_f.astype(BF16)
    high_b = (1.0 - low_f).astype(BF16)

    def block_diag(x):
        zero = jnp.zeros((width, 128), BF16)
        rows = []
        for t in range(2):
            tile = x[:, t * 128:(t + 1) * 128]
            for mask in (low_b, high_b):
                pair = [zero, zero]
                pair[t] = tile * mask
                rows.append(jnp.concatenate(pair, axis=1))
        return jnp.concatenate(rows, axis=0)

    def states(g):
        in_copy(k_hbm, kb, 0, g).wait()
        in_copy(v_hbm, vb, 1, g).wait()
        packed = []
        for i in range(blocks):
            at = slice(i * BLOCK, (i + 1) * BLOCK)
            tiles = []
            for t in range(2):
                pair_at = pl.ds(g * GROUP + 2 * t, 2)
                values = vb[pair_at, :, at].reshape(128, BLOCK)
                keys = kb[pair_at, :, at].reshape(128, BLOCK)
                both = lax.dot_general(
                    values, keys, (((1,), (1,)), ((), ())), preferred_element_type=F32
                )
                tiles.append(jnp.where(low, both[:64], both[64:]))
            packed.append(jnp.concatenate(tiles, axis=1))
        for at, (_, first, count) in enumerate(plan):
            lst[g, at] = functools.reduce(jnp.add, packed[first:first + count]).astype(BF16)
        own[g] = functools.reduce(jnp.add, packed)

    def forward_first(g):
        @pl.when(lax.rem(me, 2) == 0)
        def _():
            fwd[g] = own[g]
            state_copy(g, 0, 0).start()

    def forward_later(g):
        for m in range(1, bits):
            @pl.when(lax.rem(me, 2 << m) == (1 << m) - 1)
            def _():
                total = own[g]
                for l in range(m):
                    state_copy(g, l, 0).wait_recv()
                    total = total + rbuf[l, g]
                fwd[g] = total
                for j in reversed(range(1 << m)):
                    state_copy(g, m, j).start()

    def factor_row(head, level, at):
        return wf[level, pl.ds(head, 1), at]

    col = lax.broadcasted_iota(jnp.int32, (C, 128), 1)
    row = lax.broadcasted_iota(jnp.int32, (C, 128), 0)
    causal = (col >= row, col >= row + C)
    col_row = lax.broadcasted_iota(jnp.int32, (1, 128), 1) < C

    def local(g):
        in_copy(q_hbm, qb, 2, g).wait()
        for i in range(blocks):
            at = slice(i * BLOCK, (i + 1) * BLOCK)
            levels = [
                (s, b) for s, (b, first, count) in enumerate(plan)
                if i >> b & 1 and (i >> (b + 1)) << (b + 1) == first
            ]
            if levels:
                queries = qb[pl.ds(g * GROUP, GROUP), :, at].reshape(GROUP * width, BLOCK)
                lhs = jnp.concatenate([block_diag(lst[g, s]) for s, _ in levels], axis=0)
                reads = jnp.dot(lhs, queries, preferred_element_type=F32)
            grid = []
            for h in range(GROUP):
                head = g * GROUP + h
                scores = lax.dot_general(
                    kb[head, :, at], qb[head, :, at], (((0,), (0,)), ((), ())),
                    preferred_element_type=F32,
                )
                diag, one, two = (factor_row(head, n, at) for n in range(3))
                rows = []
                for c in range(BLOCK // C):
                    t = c // 2
                    near = slice(t * 128, (t + 1) * 128)
                    if c % 2 == 0:
                        mult = jnp.where(col_row, diag[:, near], one[:, near])
                    else:
                        mult = diag[:, near]
                    part_rows = scores[c * C:(c + 1) * C]
                    tile = jnp.where(causal[c % 2], part_rows[:, near] * mult, 0.0).astype(BF16)
                    if t == 0:
                        pair = [tile, (part_rows[:, 128:] * two[:, 128:]).astype(BF16)]
                    else:
                        pair = [jnp.zeros((C, 128), BF16), tile]
                    rows.append(jnp.concatenate(pair, axis=1))
                grid.append(jnp.concatenate(rows, axis=0))
            for h in range(GROUP):
                head = g * GROUP + h
                total = jnp.dot(vb[head, :, at], grid[h], preferred_element_type=F32)
                for n, (_, b) in enumerate(levels):
                    base = n * GROUP * 64 + h * 64
                    total = total + reads[base:base + 64] * factor_row(
                        head, b + stretch_bits + 1, at
                    )
                part[head, :, at] = total

    def far(g, m):
        @pl.when(lax.rem(me // (1 << m), 2) == 1)
        def _():
            waited = jnp.logical_and(
                lax.rem(me, 2 << m) == (2 << m) - 1, me != seq_size - 1
            )

            @pl.when(jnp.logical_not(waited))
            def _():
                state_copy(g, m, 0).wait_recv()

            lhs = block_diag(rbuf[m, g].astype(BF16))
            for i in range(blocks):
                at = slice(i * BLOCK, (i + 1) * BLOCK)
                queries = qb[pl.ds(g * GROUP, GROUP), :, at].reshape(GROUP * width, BLOCK)
                reads = jnp.dot(lhs, queries, preferred_element_type=F32)
                for h in range(GROUP):
                    head = g * GROUP + h
                    part[head, :, at] += reads[h * 64:(h + 1) * 64] * factor_row(
                        head, local_bits + m + 1, at
                    )

    def finish(g):
        sub_copy(g).wait_recv()
        heads_at = pl.ds(g * GROUP, GROUP)
        mine = part[heads_at, pl.ds(pl.multiple_of(sub * half, half), half), :]
        out[heads_at] = (mine + rsub[heads_at]).astype(BF16)

    def loop(body):
        lax.fori_loop(0, groups, lambda g, carry: (body(g), carry)[1], 0)

    states(0)
    pl.semaphore_wait(barrier, seq_size)
    forward_first(0)

    @pl.loop(1, groups)
    def _(g):
        states(g)
        forward_first(g)

    w_copy.wait()
    wf[0] = wb[0].astype(F32) * C ** (-0.5)
    for b in range(local_bits + bits):
        wf[b + 1] = wb[b + 1].astype(F32) * (2 ** b * C) ** (-0.5)

    def send(g):
        for m in range(bits):
            far(g, m)
        sub_copy(g).start()

    @pl.loop(0, groups)
    def _(g):
        local(g)
        forward_later(g)

        @pl.when(g > 0)
        def _():
            send(g - 1)

        @pl.when(g > 1)
        def _():
            finish(g - 2)

    send(groups - 1)
    if groups > 1:
        finish(groups - 2)
    finish(groups - 1)

    @pl.loop(0, groups)
    def _(g):
        sub_copy(g).wait_send()
        for m in range(bits):
            @pl.when(lax.rem(me, 2 << m) == (1 << m) - 1)
            def _():
                for j in range(1 << m):
                    state_copy(g, m, j).wait_send()


def on_device(seq_size, query_rows, key_rows, value_rows, level_weights):
    heads, width, tokens = query_rows.shape
    value_width = value_rows.shape[1]
    weights = jnp.swapaxes(level_weights, 0, 1)
    groups = heads // GROUP
    bits = seq_size.bit_length() - 1
    packed = (value_width, GROUP * width)
    hbm = pl.BlockSpec(memory_space=pltpu.HBM)
    return pl.pallas_call(
        functools.partial(kernel, seq_size),
        out_shape=jax.ShapeDtypeStruct((heads, value_width // 2, tokens), BF16),
        in_specs=[hbm] * 4,
        out_specs=pl.BlockSpec(memory_space=pltpu.VMEM),
        scratch_shapes=[
            pltpu.VMEM(query_rows.shape, BF16),
            pltpu.VMEM(key_rows.shape, BF16),
            pltpu.VMEM(value_rows.shape, BF16),
            pltpu.VMEM(weights.shape, BF16),
            pltpu.VMEM(weights.shape, F32),
            pltpu.VMEM((groups, len(local_plan(tokens))) + packed, BF16),
            pltpu.VMEM((groups,) + packed, F32),
            pltpu.VMEM((groups,) + packed, F32),
            pltpu.VMEM((bits, groups) + packed, F32),
            pltpu.VMEM((heads, value_width, tokens), F32),
            pltpu.VMEM((heads, value_width // 2, tokens), F32),
            pltpu.SemaphoreType.DMA((3, groups)),
            pltpu.SemaphoreType.DMA,
            pltpu.SemaphoreType.DMA((groups, seq_size // 2)),
            pltpu.SemaphoreType.DMA((bits, groups)),
            pltpu.SemaphoreType.DMA((groups,)),
            pltpu.SemaphoreType.DMA((groups,)),
        ],
        compiler_params=pltpu.CompilerParams(
            collective_id=0, has_side_effects=True, vmem_limit_bytes=52 * 2**20
        ),
    )(query_rows, key_rows, value_rows, weights)


def solution(mesh):
    placed = (
        P("head", "sub", ("groups", "seq")),
        P("head", "sub", ("groups", "seq")),
        P("head", None, ("groups", "seq")),
        P("head", None, ("groups", "seq")),
    )
    return jax.shard_map(
        functools.partial(on_device, mesh.shape["seq"]),
        mesh=mesh,
        in_specs=placed,
        out_specs=P("head", "sub", ("groups", "seq")),
        check_vma=False,
    )
```
